32 devices in a mesh: feat: 4 (over z), trainer: 8 (over y, x, core).
Axes of the slice: x: 2, y: 2, z: 4, core: 2. Of those that a mesh axis runs over, the one named last changes fastest.
Arguments:
- features: bfloat16 [128, 32768], P('feat', 'trainer'), may hold values from -6 to 6
- first_adjacent: int32 [4096, 15], P('trainer'), may hold values from 0 to 4095
- first_center: int32 [4096], P('trainer'), may hold values from 0 to 4095
- first_count: int32 [4096], P('trainer'), may hold values from 1 to 15
- owner_map: int32 [4096], P('trainer'), may hold values from 0 to 31, as said below
- first_root: bfloat16 [128, 1024], P('feat'), may hold values from -0.5 to 0.5
- first_near: bfloat16 [128, 1024], P('feat'), may hold values from -0.5 to 0.5
- first_bias: float32 [1024], replicated, may hold values from -3 to 3
- second_adjacent: int32 [16384, 10], P(('feat', 'trainer')), may hold values from 0 to 255, as said below
- second_center: int32 [16384], P(('feat', 'trainer')), may hold values from 0 to 255, as said below
- second_count: int32 [16384], P(('feat', 'trainer')), may hold values from 1 to 10
- second_root: bfloat16 [1024, 1024], replicated, may hold values from -0.1875 to 0.1875
- second_near: bfloat16 [1024, 1024], replicated, may hold values from -0.1875 to 0.1875
- second_bias: float32 [1024], replicated, may hold values from -3 to 3
- upstream: bfloat16 [16384, 1024], P(('feat', 'trainer')), may hold values from -0.046875 to 0.046875
Outputs:
- layer_output: bfloat16 [16384, 1024], P(('feat', 'trainer'))
- rootgrad_two: float32 [1024, 1024], replicated
- neargrad_two: float32 [1024, 1024], replicated
- biasgrad_two: float32 [1024], replicated
- rootgrad_one: float32 [128, 1024], P('feat')
- neargrad_one: float32 [128, 1024], P('feat')
- biasgrad_one: float32 [1024], replicated
The draws below stay inside these ranges and needn't reach their ends.
Inputs may be any that keep to these rules, and one draw needn't show every extreme that they name: `owner_map`: among the 512 layer-one nodes of one trainer block at most 32 name any one owner; in every draw some owner is named by exactly 32 nodes of every block, and every owner is named by some node. `second_adjacent`: every entry names a filled row of the owner's table: row s * 32 + c with c smaller than the number of nodes of block s that name this owner. `second_center`: every entry names a filled row of the owner's table, as for second_adjacent.
All inputs are finite; a program needn't handle non-finite values.
Results may differ from the reference program's by a relative error of at most 0.025.
Values may be sent and summed in bfloat16 or wider, within the bound.
A program may use at most 128 MiB of HBM per device.

```python
import jax
import jax.numpy as jnp
from jax import lax

FEAT_IN = 128
HID = 1024
FAN1 = 15
FAN2 = 10
CAP = 32
IN_DEV = 4096
L2_DEV = 512
NOWN = 32
L1_DEV = 512
SLOTS = 256
L1_TOTAL = 4096
IN_TOTAL = 32768
L2_TOTAL = 16384
N_FEAT = 4
N_TRAINER = 8


def owner_blocks(base_key):
    slot_count = NOWN * CAP
    popular = jax.random.randint(jax.random.fold_in(base_key, 11), (NOWN,), 0, 4)
    chosen_owner = jax.random.randint(jax.random.fold_in(base_key, 12), (), 0, NOWN)
    slot_ids = jnp.arange(slot_count, dtype=jnp.int32)
    slot_owner = slot_ids // CAP
    slot_place = slot_ids % CAP

    def one_source(source):
        source_key = jax.random.fold_in(jax.random.fold_in(base_key, 13), source)
        priority = jax.random.randint(source_key, (slot_count,), 0, 4096) + (3 - popular[slot_owner]) * 1024
        forced = (slot_owner == chosen_owner) | (slot_owner % N_TRAINER == source) & (slot_place == 0)
        priority = jnp.where(forced, -1, priority)
        ranking = jnp.argsort(priority * slot_count + slot_ids, stable=True)
        picked = ranking[:L1_DEV]
        shuffle = jax.random.permutation(jax.random.fold_in(source_key, 1), L1_DEV)
        return slot_owner[picked][shuffle]
    return jax.vmap(one_source)(jnp.arange(N_TRAINER, dtype=jnp.int32))


def second_slots(key):
    owners = owner_blocks(jax.random.fold_in(key, 7))
    owner_ids = jnp.arange(NOWN, dtype=jnp.int32)
    load_table = jnp.sum((owners[:, :, None] == owner_ids[None, None, :]).astype(jnp.int32), axis=1)
    load_ends = jnp.cumsum(load_table, axis=0).T
    load_starts = load_ends - load_table.T
    totals = load_ends[:, -1]
    random_bits = jax.random.randint(jax.random.fold_in(key, 21), (NOWN, L2_DEV * (FAN2 + 1)), 0, 1 << 30)
    chosen = random_bits % totals[:, None]
    source = jnp.sum((load_ends[:, None, :] <= chosen[:, :, None]).astype(jnp.int32), axis=2)
    place = chosen - jnp.take_along_axis(load_starts, source, axis=1)
    return (source * CAP + place).reshape(NOWN, L2_DEV, FAN2 + 1)


def draw_owner_map(key, part):
    return owner_blocks(jax.random.fold_in(key, 7)).reshape(-1).astype(jnp.int32)


def draw_second_adjacent(key, part):
    return second_slots(key)[:, :, :FAN2].reshape(NOWN * L2_DEV, FAN2).astype(jnp.int32)


def draw_second_center(key, part):
    return second_slots(key)[:, :, FAN2].reshape(-1).astype(jnp.int32)


def place_ends(entries, rng, low, largest):
    longest = entries.shape.index(max(entries.shape))
    spots = []
    for shift in (0, 1):
        where = [jax.random.randint(jax.random.fold_in(rng, axis), (), 0, length) for axis, length in enumerate(entries.shape)]
        where[longest] = (where[longest] + shift) % entries.shape[longest]
        spots.append(tuple(where))
    return entries.at[spots[0]].set(low).at[spots[1]].set(largest)


def block_levels(rng, shape, shards, least, high):
    level = 1.0
    for dim, blocks in shards:
        steps = jax.random.uniform(jax.random.fold_in(jax.random.fold_in(rng, 6), dim), (blocks,), jnp.float32, least / len(shards), high / len(shards))
        level = level * jnp.repeat(jnp.exp(steps), shape[dim] // blocks).reshape((-1,) + (1,) * (len(shape) - 1 - dim))
    return level


def gaussian(own_key, dims, deviation, reach, shards=(), kind=jnp.bfloat16):
    factor_of = block_levels(own_key, dims, shards, -0.22, 0.18) if shards else 1.0
    drawn = jax.random.normal(own_key, dims, jnp.float32) * deviation * factor_of
    return jnp.minimum(jnp.maximum(drawn, -reach), reach).astype(kind)


def setup_inputs(seed: int = 0) -> dict:
    keys = jax.random.split(jax.random.key(seed), 16)
    return {
        "features": gaussian(keys[0], (FEAT_IN, IN_TOTAL), 1.0, 6.0, ((0, 4), (1, 8))),
        "first_adjacent": place_ends(jax.random.randint(keys[1], (L1_TOTAL, FAN1), 0, IN_DEV), jax.random.fold_in(keys[1], 1), 0, IN_DEV - 1).astype(jnp.int32),
        "first_center": place_ends(jax.random.randint(keys[2], (L1_TOTAL,), 0, IN_DEV), jax.random.fold_in(keys[2], 1), 0, IN_DEV - 1).astype(jnp.int32),
        "first_count": place_ends(jax.random.randint(keys[3], (L1_TOTAL,), 1, FAN1 + 1), jax.random.fold_in(keys[3], 1), 1, FAN1).astype(jnp.int32),
        "owner_map": draw_owner_map(jax.random.fold_in(keys[15], 71), 0),
        "first_root": gaussian(keys[5], (FEAT_IN, HID), FEAT_IN ** -0.5, 0.5, ((0, 4),)),
        "first_near": gaussian(keys[6], (FEAT_IN, HID), FEAT_IN ** -0.5, 0.5, ((0, 4),)),
        "first_bias": gaussian(keys[7], (HID,), 0.5, 3.0, (), jnp.float32),
        "second_adjacent": draw_second_adjacent(jax.random.fold_in(keys[15], 71), 0),
        "second_center": draw_second_center(jax.random.fold_in(keys[15], 71), 0),
        "second_count": place_ends(jax.random.randint(keys[10], (L2_TOTAL,), 1, FAN2 + 1), jax.random.fold_in(keys[10], 1), 1, FAN2).astype(jnp.int32),
        "second_root": gaussian(keys[11], (HID, HID), HID ** -0.5, 0.1875),
        "second_near": gaussian(keys[12], (HID, HID), HID ** -0.5, 0.1875),
        "second_bias": gaussian(keys[13], (HID,), 0.5, 3.0, (), jnp.float32),
        "upstream": gaussian(keys[14], (L2_TOTAL, HID), (1.0 / L2_TOTAL ** 0.5), 0.046875, ((0, 32),)),
    }


def reference(features, first_adjacent, first_center, first_count, owner_map, first_root, first_near, first_bias, second_adjacent, second_center, second_count, second_root, second_near, second_bias, upstream):
    block_width = FEAT_IN // N_FEAT
    node_ids = jnp.arange(L1_TOTAL, dtype=jnp.int32)
    sources = node_ids // L1_DEV
    columns = features.T
    offsets = sources * IN_DEV
    center_rows = jnp.take(columns, offsets + first_center, axis=0)
    near_total = jnp.zeros((L1_TOTAL, FEAT_IN), jnp.float32)
    for column in range(FAN1):
        picked = jnp.take(columns, offsets + first_adjacent[:, column], axis=0).astype(jnp.float32)
        near_total = near_total + jnp.where((column < first_count)[:, None], picked, jnp.float32(0.0))
    near_rows = (near_total / first_count.astype(jnp.float32)[:, None]).astype(jnp.bfloat16)
    pre_one = jnp.zeros((L1_TOTAL, HID), jnp.float32) + first_bias
    for quarter in range(N_FEAT):
        low = quarter * block_width
        high = low + block_width
        part = jnp.dot(center_rows[:, low:high], first_root[low:high], preferred_element_type=jnp.float32)
        part = part + jnp.dot(near_rows[:, low:high], first_near[low:high], preferred_element_type=jnp.float32)
        pre_one = pre_one + part.astype(jnp.bfloat16).astype(jnp.float32)
    hidden_one = jax.nn.softplus(pre_one).astype(jnp.bfloat16)
    empty_row = jax.nn.softplus(first_bias).astype(jnp.bfloat16)[None, :]
    hidden_pad = jnp.concatenate([hidden_one, empty_row], axis=0)
    onehot = (owner_map.reshape(N_TRAINER, L1_DEV, 1) == jnp.arange(NOWN, dtype=jnp.int32)[None, None, :]).astype(jnp.int32)
    slot_rank = jnp.sum((jnp.cumsum(onehot, axis=1) - onehot) * onehot, axis=2).reshape(-1)
    position = sources * CAP + slot_rank
    table_index = jnp.full((NOWN, SLOTS), L1_TOTAL, jnp.int32).at[owner_map, position].set(node_ids)

    def owner_step(totals, inputs):
        index_row, adjacent, center, count, grad_out = inputs
        hidden_table = jnp.take(hidden_pad, index_row, axis=0)
        root_rows = jnp.take(hidden_table, center, axis=0)
        near_sum = jnp.zeros((L2_DEV, HID), jnp.float32)
        for column in range(FAN2):
            picked = jnp.take(hidden_table, adjacent[:, column], axis=0).astype(jnp.float32)
            near_sum = near_sum + jnp.where((column < count)[:, None], picked, jnp.float32(0.0))
        divisor = count.astype(jnp.float32)[:, None]
        near_two = (near_sum / divisor).astype(jnp.bfloat16)
        pre_two = jnp.dot(root_rows, second_root, preferred_element_type=jnp.float32)
        pre_two = pre_two + jnp.dot(near_two, second_near, preferred_element_type=jnp.float32) + second_bias
        gate = jax.nn.sigmoid(pre_two)
        output_rows = (pre_two * gate).astype(jnp.bfloat16)
        slope_two = (grad_out.astype(jnp.float32) * gate * (1.0 + pre_two * (1.0 - gate))).astype(jnp.bfloat16)
        root_grad = jnp.dot(root_rows.T, slope_two, preferred_element_type=jnp.float32)
        near_grad = jnp.dot(near_two.T, slope_two, preferred_element_type=jnp.float32)
        bias_grad = jnp.sum(slope_two.astype(jnp.float32), axis=0)
        back_root = jnp.dot(slope_two, second_root.T, preferred_element_type=jnp.float32).astype(jnp.bfloat16)
        back_near = (jnp.dot(slope_two, second_near.T, preferred_element_type=jnp.float32) / divisor).astype(jnp.bfloat16)
        table_grad = jnp.zeros((SLOTS, HID), jnp.float32).at[center].add(back_root.astype(jnp.float32))
        usable = jnp.arange(FAN2, dtype=jnp.int32)[None, :] < count[:, None]
        targets = jnp.where(usable, adjacent, SLOTS).reshape(-1)
        spread = jnp.broadcast_to(back_near.astype(jnp.float32)[:, None, :], (L2_DEV, FAN2, HID)).reshape(L2_DEV * FAN2, HID)
        table_grad = table_grad.at[targets].add(spread, mode="drop")
        pre_grad = (table_grad * (1.0 - jnp.exp(-hidden_table.astype(jnp.float32)))).astype(jnp.bfloat16)
        totals = (totals[0] + root_grad, totals[1] + near_grad, totals[2] + bias_grad)
        return totals, (output_rows, pre_grad)

    start = (jnp.zeros((HID, HID), jnp.float32), jnp.zeros((HID, HID), jnp.float32), jnp.zeros((HID,), jnp.float32))
    inputs = (table_index, second_adjacent.reshape(NOWN, L2_DEV, FAN2), second_center.reshape(NOWN, L2_DEV), second_count.reshape(NOWN, L2_DEV), upstream.reshape(NOWN, L2_DEV, HID))
    totals, stacked = lax.scan(owner_step, start, inputs)
    layer_output = stacked[0].reshape(L2_TOTAL, HID)
    node_grad = stacked[1][owner_map, position]
    rootgrad_one = jnp.dot(center_rows.T, node_grad, preferred_element_type=jnp.float32)
    neargrad_one = jnp.dot(near_rows.T, node_grad, preferred_element_type=jnp.float32)
    biasgrad_one = jnp.sum(node_grad.astype(jnp.float32), axis=0)
    return layer_output, totals[0], totals[1], totals[2], rootgrad_one, neargrad_one, biasgrad_one
```

```python
import functools

import jax
import jax.numpy as jnp
from jax import lax
from jax.experimental import pallas as pl
from jax.experimental.pallas import tpu as pltpu
from jax.sharding import PartitionSpec as P

CAP = 32


CHUNK = 256
ROWS = 16
LANES = 128


def select_kernel(fanout, ids_ref, feat_ref, out_ref, picks):
    width, inputs = feat_ref.shape
    nodes = ids_ref.shape[1]
    out_ref[...] = jnp.zeros_like(out_ref)
    inner = (
        lax.broadcasted_iota(jnp.int32, (CHUNK // ROWS, ROWS, LANES), 0) * ROWS
        + lax.broadcasted_iota(jnp.int32, (CHUNK // ROWS, ROWS, LANES), 1)
    ).astype(jnp.float32).astype(jnp.bfloat16)
    one, zero = jnp.bfloat16(1.0), jnp.bfloat16(0.0)

    def chunk_step(chunk, carry):
        start = pl.multiple_of(chunk * CHUNK, CHUNK)
        for tile in range(nodes // LANES):
            lanes = slice(tile * LANES, (tile + 1) * LANES)
            local_ids = ids_ref[:, lanes] - start
            local_ids = jnp.where((local_ids >= 0) & (local_ids < CHUNK), local_ids, -1)
            local_ids = local_ids.astype(jnp.float32)
            total = None
            for column in range(fanout + 1):
                row = jnp.broadcast_to(local_ids[column : column + 1], (ROWS, LANES))
                hit = jnp.where(inner == row.astype(jnp.bfloat16)[None], one, zero)
                if column == fanout:
                    picks[:, nodes + tile * LANES : nodes + (tile + 1) * LANES] = hit.reshape(
                        CHUNK, LANES
                    )
                else:
                    total = hit if total is None else total + hit
            picks[:, lanes] = total.reshape(CHUNK, LANES)
        out_ref[...] += jnp.dot(
            feat_ref[:, pl.ds(start, CHUNK)], picks[...], preferred_element_type=jnp.float32
        )
        return carry

    lax.fori_loop(0, inputs // CHUNK, chunk_step, 0)


def select(features, adjacent, center, count):
    width, inputs = features.shape
    nodes, fanout = adjacent.shape
    columns = jnp.arange(fanout, dtype=jnp.int32)[None, :]
    ids = jnp.where(columns < count[:, None], adjacent, -1)
    ids = jnp.concatenate([ids, center[:, None]], axis=1).T
    block = 512
    steps = nodes // block
    out = pl.pallas_call(
        functools.partial(select_kernel, fanout),
        grid=(steps,),
        in_specs=[
            pl.BlockSpec((fanout + 1, block), lambda i: (0, i)),
            pl.BlockSpec((width, inputs), lambda i: (0, 0)),
        ],
        out_specs=pl.BlockSpec((width, 2 * block), lambda i: (0, i)),
        out_shape=jax.ShapeDtypeStruct((width, 2 * nodes), jnp.float32),
        scratch_shapes=[pltpu.VMEM((CHUNK, 2 * block), jnp.bfloat16)],
        cost_estimate=pl.CostEstimate(
            flops=40 * nodes * inputs * width, bytes_accessed=width * inputs * 2, transcendentals=0
        ),
    )(ids, features)
    out = out.reshape(width, steps, 2, block)
    return out[:, :, 1].reshape(width, nodes), out[:, :, 0].reshape(width, nodes)


def cross_rows(left, right):
    return lax.dot_general(
        left, right, (((0,), (0,)), ((), ())), preferred_element_type=jnp.float32
    )


def cross_cols(left, right):
    return lax.dot_general(
        left, right, (((1,), (1,)), ((), ())), preferred_element_type=jnp.float32
    )


def local(
    features,
    first_adjacent,
    first_center,
    first_count,
    owner_map,
    first_root,
    first_near,
    first_bias,
    second_adjacent,
    second_center,
    second_count,
    second_root,
    second_near,
    second_bias,
    upstream,
):
    feat_size = lax.axis_size("feat")
    trainers = lax.axis_size("trainer")
    owners_all = feat_size * trainers
    node_count = owner_map.shape[0]
    block_width = features.shape[0]
    slot_total = owners_all * CAP
    slots = trainers * CAP
    node_ids = jnp.arange(node_count, dtype=jnp.int32)
    earlier = (owner_map[:, None] == owner_map[None, :]) & (node_ids[:, None] < node_ids[None, :])
    slot_rank = jnp.sum(earlier.astype(jnp.int32), axis=0)
    position = owner_map * CAP + slot_rank
    own_cols, near_sum = select(features, first_adjacent, first_center, first_count)
    near_cols = (near_sum / first_count.astype(jnp.float32)[None, :]).astype(jnp.bfloat16)
    node_cols = jnp.concatenate([own_cols.astype(jnp.bfloat16), near_cols], axis=0)
    to_slot = (position[:, None] == jnp.arange(slot_total, dtype=jnp.int32)[None, :]).astype(
        jnp.bfloat16
    )
    packed = jnp.dot(node_cols, to_slot, preferred_element_type=jnp.float32).astype(jnp.bfloat16)
    packed = packed.reshape(2 * block_width, owners_all, CAP)
    arrived = lax.all_to_all(packed, ("feat", "trainer"), split_axis=1, concat_axis=1, tiled=True)
    arrived = (
        arrived.reshape(2, block_width, feat_size, trainers, CAP)
        .transpose(0, 2, 1, 3, 4)
        .reshape(2 * feat_size * block_width, slots)
    )
    root_all, near_all = (
        lax.all_gather(first_root, "feat", axis=0, tiled=True),
        lax.all_gather(first_near, "feat", axis=0, tiled=True),
    )
    pre_one = cross_rows(arrived, jnp.concatenate([root_all, near_all], axis=0)) + first_bias
    hidden_table = jax.nn.softplus(pre_one).astype(jnp.bfloat16)
    slot_ids = jnp.arange(slots, dtype=jnp.int32)
    root_pick = (second_center[:, None] == slot_ids[None, :]).astype(jnp.bfloat16)
    root_rows = jnp.dot(root_pick, hidden_table, preferred_element_type=jnp.float32).astype(
        jnp.bfloat16
    )
    multiples = jnp.zeros((second_center.shape[0], slots), jnp.float32)
    for column in range(second_adjacent.shape[1]):
        hits = (column < second_count)[:, None] & (
            second_adjacent[:, column : column + 1] == slot_ids[None, :]
        )
        multiples = multiples + jnp.where(hits, jnp.float32(1.0), jnp.float32(0.0))
    multiples = multiples.astype(jnp.bfloat16)
    divisor = second_count.astype(jnp.float32)[:, None]
    near_two = (
        jnp.dot(multiples, hidden_table, preferred_element_type=jnp.float32) / divisor
    ).astype(jnp.bfloat16)
    pre_two = jnp.dot(root_rows, second_root, preferred_element_type=jnp.float32)
    pre_two = (
        pre_two + jnp.dot(near_two, second_near, preferred_element_type=jnp.float32) + second_bias
    )
    gate = jax.nn.sigmoid(pre_two)
    layer_output = (pre_two * gate).astype(jnp.bfloat16)
    slope_two = (upstream.astype(jnp.float32) * gate * (1.0 + pre_two * (1.0 - gate))).astype(
        jnp.bfloat16
    )
    both = jnp.concatenate([root_rows, near_two], axis=1)
    grad_two = lax.psum(cross_rows(both, slope_two).astype(jnp.bfloat16), ("feat", "trainer"))
    back_root = cross_cols(slope_two, second_root).astype(jnp.bfloat16)
    back_near = (cross_cols(slope_two, second_near) / divisor).astype(jnp.bfloat16)
    table_grad = cross_rows(root_pick, back_root) + cross_rows(multiples, back_near)
    pre_grad = (table_grad * (1.0 - jnp.exp(-hidden_table.astype(jnp.float32)))).astype(
        jnp.bfloat16
    )
    grad_one = jnp.dot(arrived, pre_grad, preferred_element_type=jnp.float32)
    grad_one = grad_one.astype(jnp.bfloat16).reshape(2, feat_size, block_width, -1)
    grad_one = lax.psum(grad_one, ("feat", "trainer"))
    grad_one = lax.dynamic_index_in_dim(grad_one, lax.axis_index("feat"), 1, keepdims=False)
    biases = jnp.stack(
        [
            jnp.sum(slope_two.astype(jnp.float32), axis=0),
            jnp.sum(pre_grad.astype(jnp.float32), axis=0),
        ]
    )
    biasgrad_two, biasgrad_one = lax.psum(biases, ("feat", "trainer"))
    grad_two = grad_two.astype(jnp.float32).reshape(2, -1, grad_two.shape[1])
    rootgrad_two, neargrad_two = grad_two
    rootgrad_one, neargrad_one = grad_one.astype(jnp.float32)
    return (
        layer_output,
        rootgrad_two,
        neargrad_two,
        biasgrad_two,
        rootgrad_one,
        neargrad_one,
        biasgrad_one,
    )


def solution(mesh):
    return jax.shard_map(
        local,
        mesh=mesh,
        in_specs=(
            P("feat", "trainer"),
            P("trainer", None),
            P("trainer"),
            P("trainer"),
            P("trainer"),
            P("feat", None),
            P("feat", None),
            P(),
            P(("feat", "trainer"), None),
            P(("feat", "trainer")),
            P(("feat", "trainer")),
            P(),
            P(),
            P(),
            P(("feat", "trainer"), None),
        ),
        out_specs=(
            P(("feat", "trainer"), None),
            P(),
            P(),
            P(),
            P("feat", None),
            P("feat", None),
            P(),
        ),
        check_vma=False,
    )
```

```python
import functools

import jax
import jax.numpy as jnp
from jax import lax
from jax.experimental import pallas as pl
from jax.experimental.pallas import tpu as pltpu
from jax.sharding import PartitionSpec as P

CAP = 32


def links():
    def bits(axis):
        return [(axis, bit) for bit in range(lax.axis_size(axis).bit_length() - 1)]

    across, feat = bits("trainer"), bits("feat")
    core, rest = across[:1], across[1:]
    low, high = rest[: len(rest) // 2], rest[len(rest) // 2 :]
    return core, low, high, feat


def exchange(rows, link):
    axis, bit = link
    pairs = [(i, i ^ (1 << bit)) for i in range(lax.axis_size(axis))]
    return lax.ppermute(rows, axis, pairs)


def side(link):
    axis, bit = link
    return (lax.axis_index(axis) >> bit) & 1


def scatter_step(rows, link):
    half = rows.shape[0] // 2
    mine = side(link)
    kept = lax.dynamic_slice_in_dim(rows, mine * half, half, 0)
    got = exchange(lax.dynamic_slice_in_dim(rows, (1 - mine) * half, half, 0), link)
    return (kept.astype(jnp.float32) + got.astype(jnp.float32)).astype(jnp.bfloat16)


def gather_step(rows, link):
    got = exchange(rows, link)
    first = side(link) == 0
    return jnp.concatenate([jnp.where(first, rows, got), jnp.where(first, got, rows)], axis=0)


def sum_parts(parts, orders):
    steps = len(orders[0])
    for step in range(steps):
        parts = [scatter_step(part, order[step]) for part, order in zip(parts, orders)]
    for step in reversed(range(steps)):
        parts = [gather_step(part, order[step]) for part, order in zip(parts, orders)]
    return parts


CHUNK = 256
ROWS = 16
LANES = 128


def select_kernel(fanout, ids_ref, feat_ref, out_ref, picks):
    width, inputs = feat_ref.shape
    nodes = ids_ref.shape[1]
    out_ref[...] = jnp.zeros_like(out_ref)
    inner = (
        lax.broadcasted_iota(jnp.int32, (CHUNK // ROWS, ROWS, LANES), 0) * ROWS
        + lax.broadcasted_iota(jnp.int32, (CHUNK // ROWS, ROWS, LANES), 1)
    ).astype(jnp.float32).astype(jnp.bfloat16)
    one, zero = jnp.bfloat16(1.0), jnp.bfloat16(0.0)

    def chunk_step(chunk, carry):
        start = pl.multiple_of(chunk * CHUNK, CHUNK)
        for tile in range(nodes // LANES):
            lanes = slice(tile * LANES, (tile + 1) * LANES)
            local_ids = ids_ref[:, lanes] - start
            local_ids = jnp.where((local_ids >= 0) & (local_ids < CHUNK), local_ids, -1)
            local_ids = local_ids.astype(jnp.float32)
            total = None
            for column in range(fanout + 1):
                row = jnp.broadcast_to(local_ids[column : column + 1], (ROWS, LANES))
                hit = jnp.where(inner == row.astype(jnp.bfloat16)[None], one, zero)
                if column == fanout:
                    picks[:, nodes + tile * LANES : nodes + (tile + 1) * LANES] = hit.reshape(
                        CHUNK, LANES
                    )
                else:
                    total = hit if total is None else total + hit
            picks[:, lanes] = total.reshape(CHUNK, LANES)
        out_ref[...] += jnp.dot(
            feat_ref[:, pl.ds(start, CHUNK)], picks[...], preferred_element_type=jnp.float32
        )
        return carry

    lax.fori_loop(0, inputs // CHUNK, chunk_step, 0)


def select(features, adjacent, center, count):
    width, inputs = features.shape
    nodes, fanout = adjacent.shape
    columns = jnp.arange(fanout, dtype=jnp.int32)[None, :]
    ids = jnp.where(columns < count[:, None], adjacent, -1)
    ids = jnp.concatenate([ids, center[:, None]], axis=1).T
    block = 512
    steps = nodes // block
    out = pl.pallas_call(
        functools.partial(select_kernel, fanout),
        grid=(steps,),
        in_specs=[
            pl.BlockSpec((fanout + 1, block), lambda i: (0, i)),
            pl.BlockSpec((width, inputs), lambda i: (0, 0)),
        ],
        out_specs=pl.BlockSpec((width, 2 * block), lambda i: (0, i)),
        out_shape=jax.ShapeDtypeStruct((width, 2 * nodes), jnp.float32),
        scratch_shapes=[pltpu.VMEM((CHUNK, 2 * block), jnp.bfloat16)],
        cost_estimate=pl.CostEstimate(
            flops=40 * nodes * inputs * width, bytes_accessed=width * inputs * 2, transcendentals=0
        ),
    )(ids, features)
    out = out.reshape(width, steps, 2, block)
    return out[:, :, 1].reshape(width, nodes), out[:, :, 0].reshape(width, nodes)


def cross_rows(left, right):
    return lax.dot_general(
        left, right, (((0,), (0,)), ((), ())), preferred_element_type=jnp.float32
    )


def cross_cols(left, right):
    return lax.dot_general(
        left, right, (((1,), (1,)), ((), ())), preferred_element_type=jnp.float32
    )


def local(
    features,
    first_adjacent,
    first_center,
    first_count,
    owner_map,
    first_root,
    first_near,
    first_bias,
    second_adjacent,
    second_center,
    second_count,
    second_root,
    second_near,
    second_bias,
    upstream,
):
    feat_size = lax.axis_size("feat")
    trainers = lax.axis_size("trainer")
    owners_all = feat_size * trainers
    node_count = owner_map.shape[0]
    block_width = features.shape[0]
    slot_total = owners_all * CAP
    slots = trainers * CAP
    core, low, high, feat = links()
    weights = jnp.concatenate([first_root, first_near], axis=0)
    for link in feat:
        weights = gather_step(weights, link)
    node_ids = jnp.arange(node_count, dtype=jnp.int32)
    earlier = (owner_map[:, None] == owner_map[None, :]) & (node_ids[:, None] < node_ids[None, :])
    slot_rank = jnp.sum(earlier.astype(jnp.int32), axis=0)
    position = owner_map * CAP + slot_rank
    own_cols, near_sum = select(features, first_adjacent, first_center, first_count)
    near_cols = (near_sum / first_count.astype(jnp.float32)[None, :]).astype(jnp.bfloat16)
    node_cols = jnp.concatenate([own_cols.astype(jnp.bfloat16), near_cols], axis=0)
    to_slot = (position[:, None] == jnp.arange(slot_total, dtype=jnp.int32)[None, :]).astype(
        jnp.bfloat16
    )
    packed = jnp.dot(node_cols, to_slot, preferred_element_type=jnp.float32).astype(jnp.bfloat16)
    packed = packed.reshape(2 * block_width, owners_all, CAP)
    arrived = lax.all_to_all(packed, ("feat", "trainer"), split_axis=1, concat_axis=1, tiled=True)
    arrived = (
        arrived.reshape(2, block_width, feat_size, trainers, CAP)
        .transpose(2, 0, 1, 3, 4)
        .reshape(2 * feat_size * block_width, slots)
    )
    pre_one = cross_rows(arrived, weights) + first_bias
    hidden_table = jax.nn.softplus(pre_one).astype(jnp.bfloat16)
    slot_ids = jnp.arange(slots, dtype=jnp.int32)
    root_pick = (second_center[:, None] == slot_ids[None, :]).astype(jnp.bfloat16)
    root_rows = jnp.dot(root_pick, hidden_table, preferred_element_type=jnp.float32).astype(
        jnp.bfloat16
    )
    multiples = jnp.zeros((second_center.shape[0], slots), jnp.float32)
    for column in range(second_adjacent.shape[1]):
        hits = (column < second_count)[:, None] & (
            second_adjacent[:, column : column + 1] == slot_ids[None, :]
        )
        multiples = multiples + jnp.where(hits, jnp.float32(1.0), jnp.float32(0.0))
    multiples = multiples.astype(jnp.bfloat16)
    divisor = second_count.astype(jnp.float32)[:, None]
    near_two = (
        jnp.dot(multiples, hidden_table, preferred_element_type=jnp.float32) / divisor
    ).astype(jnp.bfloat16)
    pre_two = jnp.dot(root_rows, second_root, preferred_element_type=jnp.float32)
    pre_two = (
        pre_two + jnp.dot(near_two, second_near, preferred_element_type=jnp.float32) + second_bias
    )
    gate = jax.nn.sigmoid(pre_two)
    layer_output = (pre_two * gate).astype(jnp.bfloat16)
    slope_two = (upstream.astype(jnp.float32) * gate * (1.0 + pre_two * (1.0 - gate))).astype(
        jnp.bfloat16
    )
    both = jnp.concatenate([root_rows, near_two], axis=1)
    grad_two = cross_rows(both, slope_two).astype(jnp.bfloat16)
    units = grad_two.shape[0] // owners_all
    ends = [(units * part // 3) * owners_all for part in range(4)]
    grad_two = sum_parts(
        [grad_two[ends[part] : ends[part + 1]] for part in range(3)],
        [core + low + high + feat, core + high + feat + low, core + feat + low + high],
    )
    grad_two = jnp.concatenate(grad_two, axis=0)
    back_root = cross_cols(slope_two, second_root).astype(jnp.bfloat16)
    back_near = (cross_cols(slope_two, second_near) / divisor).astype(jnp.bfloat16)
    table_grad = cross_rows(root_pick, back_root) + cross_rows(multiples, back_near)
    pre_grad = (table_grad * (1.0 - jnp.exp(-hidden_table.astype(jnp.float32)))).astype(
        jnp.bfloat16
    )
    grad_one = jnp.dot(arrived, pre_grad, preferred_element_type=jnp.float32)
    grad_one = grad_one.astype(jnp.bfloat16)
    for link in reversed(feat):
        grad_one = scatter_step(grad_one, link)
    (grad_one,) = sum_parts([grad_one], [core + low + high])
    grad_one = grad_one.reshape(2, block_width, -1)
    biases = jnp.stack(
        [
            jnp.sum(slope_two.astype(jnp.float32), axis=0),
            jnp.sum(pre_grad.astype(jnp.float32), axis=0),
        ]
    )
    for link in core + low + high + feat:
        biases = biases + exchange(biases, link)
    biasgrad_two, biasgrad_one = biases
    grad_two = grad_two.astype(jnp.float32).reshape(2, -1, grad_two.shape[1])
    rootgrad_two, neargrad_two = grad_two
    rootgrad_one, neargrad_one = grad_one.astype(jnp.float32)
    return (
        layer_output,
        rootgrad_two,
        neargrad_two,
        biasgrad_two,
        rootgrad_one,
        neargrad_one,
        biasgrad_one,
    )


def solution(mesh):
    return jax.shard_map(
        local,
        mesh=mesh,
        in_specs=(
            P("feat", "trainer"),
            P("trainer", None),
            P("trainer"),
            P("trainer"),
            P("trainer"),
            P("feat", None),
            P("feat", None),
            P(),
            P(("feat", "trainer"), None),
            P(("feat", "trainer")),
            P(("feat", "trainer")),
            P(),
            P(),
            P(),
            P(("feat", "trainer"), None),
        ),
        out_specs=(
            P(("feat", "trainer"), None),
            P(),
            P(),
            P(),
            P("feat", None),
            P("feat", None),
            P(),
        ),
        check_vma=False,
    )
```

```python
import functools

import jax
import jax.numpy as jnp
from jax import lax
from jax.experimental import pallas as pl
from jax.experimental.pallas import tpu as pltpu
from jax.sharding import PartitionSpec as P

CAP = 32


def links():
    def bits(axis):
        return [(axis, bit) for bit in range(lax.axis_size(axis).bit_length() - 1)]

    across, feat = bits("trainer"), bits("feat")
    core, rest = across[:1], across[1:]
    low, high = rest[: len(rest) // 2], rest[len(rest) // 2 :]
    return core, low, high, feat


def exchange(rows, link):
    axis, bit = link
    pairs = [(i, i ^ (1 << bit)) for i in range(lax.axis_size(axis))]
    return lax.ppermute(rows, axis, pairs)


def side(link):
    axis, bit = link
    return (lax.axis_index(axis) >> bit) & 1


def scatter_step(rows, link):
    half = rows.shape[0] // 2
    mine = side(link)
    kept = lax.dynamic_slice_in_dim(rows, mine * half, half, 0)
    got = exchange(lax.dynamic_slice_in_dim(rows, (1 - mine) * half, half, 0), link)
    return (kept.astype(jnp.float32) + got.astype(jnp.float32)).astype(jnp.bfloat16)


def gather_step(rows, link):
    got = exchange(rows, link)
    first = side(link) == 0
    return jnp.concatenate([jnp.where(first, rows, got), jnp.where(first, got, rows)], axis=0)


def sum_parts(parts, orders):
    steps = len(orders[0])
    for step in range(steps):
        parts = [scatter_step(part, order[step]) for part, order in zip(parts, orders)]
    for step in reversed(range(steps)):
        parts = [gather_step(part, order[step]) for part, order in zip(parts, orders)]
    return parts


CHUNK = 256
ROWS = 16
LANES = 128


def select_kernel(fanout, ids_ref, feat_ref, out_ref, picks):
    width, inputs = feat_ref.shape
    nodes = ids_ref.shape[1]
    out_ref[...] = jnp.zeros_like(out_ref)
    inner = (
        lax.broadcasted_iota(jnp.int32, (CHUNK // ROWS, ROWS, LANES), 0) * ROWS
        + lax.broadcasted_iota(jnp.int32, (CHUNK // ROWS, ROWS, LANES), 1)
    ).astype(jnp.float32).astype(jnp.bfloat16)
    one, zero = jnp.bfloat16(1.0), jnp.bfloat16(0.0)

    def chunk_step(chunk, carry):
        start = pl.multiple_of(chunk * CHUNK, CHUNK)
        for tile in range(nodes // LANES):
            lanes = slice(tile * LANES, (tile + 1) * LANES)
            local_ids = ids_ref[:, lanes] - start
            local_ids = jnp.where((local_ids >= 0) & (local_ids < CHUNK), local_ids, -1)
            local_ids = local_ids.astype(jnp.float32)
            total = None
            for column in range(fanout + 1):
                row = jnp.broadcast_to(local_ids[column : column + 1], (ROWS, LANES))
                hit = jnp.where(inner == row.astype(jnp.bfloat16)[None], one, zero)
                if column == fanout:
                    picks[:, nodes + tile * LANES : nodes + (tile + 1) * LANES] = hit.reshape(
                        CHUNK, LANES
                    )
                else:
                    total = hit if total is None else total + hit
            picks[:, lanes] = total.reshape(CHUNK, LANES)
        out_ref[...] += jnp.dot(
            feat_ref[:, pl.ds(start, CHUNK)], picks[...], preferred_element_type=jnp.float32
        )
        return carry

    lax.fori_loop(0, inputs // CHUNK, chunk_step, 0)


def select(features, adjacent, center, count):
    width, inputs = features.shape
    nodes, fanout = adjacent.shape
    columns = jnp.arange(fanout, dtype=jnp.int32)[None, :]
    ids = jnp.where(columns < count[:, None], adjacent, -1)
    ids = jnp.concatenate([ids, center[:, None]], axis=1).T
    block = 512
    steps = nodes // block
    out = pl.pallas_call(
        functools.partial(select_kernel, fanout),
        grid=(steps,),
        in_specs=[
            pl.BlockSpec((fanout + 1, block), lambda i: (0, i)),
            pl.BlockSpec((width, inputs), lambda i: (0, 0)),
        ],
        out_specs=pl.BlockSpec((width, 2 * block), lambda i: (0, i)),
        out_shape=jax.ShapeDtypeStruct((width, 2 * nodes), jnp.float32),
        scratch_shapes=[pltpu.VMEM((CHUNK, 2 * block), jnp.bfloat16)],
        cost_estimate=pl.CostEstimate(
            flops=40 * nodes * inputs * width, bytes_accessed=width * inputs * 2, transcendentals=0
        ),
    )(ids, features)
    out = out.reshape(width, steps, 2, block)
    return out[:, :, 1].reshape(width, nodes), out[:, :, 0].reshape(width, nodes)


def cross_rows(left, right):
    return lax.dot_general(
        left, right, (((0,), (0,)), ((), ())), preferred_element_type=jnp.float32
    )


def cross_cols(left, right):
    return lax.dot_general(
        left, right, (((1,), (1,)), ((), ())), preferred_element_type=jnp.float32
    )


def local(
    features,
    first_adjacent,
    first_center,
    first_count,
    owner_map,
    first_root,
    first_near,
    first_bias,
    second_adjacent,
    second_center,
    second_count,
    second_root,
    second_near,
    second_bias,
    upstream,
):
    feat_size = lax.axis_size("feat")
    trainers = lax.axis_size("trainer")
    owners_all = feat_size * trainers
    node_count = owner_map.shape[0]
    block_width = features.shape[0]
    slot_total = owners_all * CAP
    slots = trainers * CAP
    core, low, high, feat = links()
    weights = jnp.concatenate([first_root, first_near], axis=0)
    place, depth = lax.axis_index("feat"), weights.shape[0]
    gathered = jnp.zeros((feat_size * depth, weights.shape[1]), weights.dtype)
    for shift in range(feat_size):
        pairs = [(i, (i + shift) % feat_size) for i in range(feat_size)]
        piece = lax.ppermute(weights, "feat", pairs) if shift else weights
        source = (place - shift + feat_size) % feat_size
        gathered = lax.dynamic_update_slice_in_dim(gathered, piece, source * depth, 0)
    weights = gathered
    node_ids = jnp.arange(node_count, dtype=jnp.int32)
    earlier = (owner_map[:, None] == owner_map[None, :]) & (node_ids[:, None] < node_ids[None, :])
    slot_rank = jnp.sum(earlier.astype(jnp.int32), axis=0)
    position = owner_map * CAP + slot_rank
    own_cols, near_sum = select(features, first_adjacent, first_center, first_count)
    near_cols = (near_sum / first_count.astype(jnp.float32)[None, :]).astype(jnp.bfloat16)
    node_cols = jnp.concatenate([own_cols.astype(jnp.bfloat16), near_cols], axis=0)
    to_slot = (position[:, None] == jnp.arange(slot_total, dtype=jnp.int32)[None, :]).astype(
        jnp.bfloat16
    )
    packed = jnp.dot(node_cols, to_slot, preferred_element_type=jnp.float32).astype(jnp.bfloat16)
    packed = packed.reshape(2 * block_width, owners_all, CAP)
    arrived = lax.all_to_all(packed, ("feat", "trainer"), split_axis=1, concat_axis=1, tiled=True)
    arrived = (
        arrived.reshape(2, block_width, feat_size, trainers, CAP)
        .transpose(2, 0, 1, 3, 4)
        .reshape(2 * feat_size * block_width, slots)
    )
    pre_one = cross_rows(arrived, weights) + first_bias
    hidden_table = jax.nn.softplus(pre_one).astype(jnp.bfloat16)
    slot_ids = jnp.arange(slots, dtype=jnp.int32)
    root_pick = (second_center[:, None] == slot_ids[None, :]).astype(jnp.bfloat16)
    root_rows = jnp.dot(root_pick, hidden_table, preferred_element_type=jnp.float32).astype(
        jnp.bfloat16
    )
    multiples = jnp.zeros((second_center.shape[0], slots), jnp.float32)
    for column in range(second_adjacent.shape[1]):
        hits = (column < second_count)[:, None] & (
            second_adjacent[:, column : column + 1] == slot_ids[None, :]
        )
        multiples = multiples + jnp.where(hits, jnp.float32(1.0), jnp.float32(0.0))
    multiples = multiples.astype(jnp.bfloat16)
    divisor = second_count.astype(jnp.float32)[:, None]
    near_two = (
        jnp.dot(multiples, hidden_table, preferred_element_type=jnp.float32) / divisor
    ).astype(jnp.bfloat16)
    pre_two = jnp.dot(root_rows, second_root, preferred_element_type=jnp.float32)
    pre_two = (
        pre_two + jnp.dot(near_two, second_near, preferred_element_type=jnp.float32) + second_bias
    )
    gate = jax.nn.sigmoid(pre_two)
    layer_output = (pre_two * gate).astype(jnp.bfloat16)
    slope_two = (upstream.astype(jnp.float32) * gate * (1.0 + pre_two * (1.0 - gate))).astype(
        jnp.bfloat16
    )
    both = jnp.concatenate([root_rows, near_two], axis=1)
    grad_two = cross_rows(both, slope_two).astype(jnp.bfloat16)
    back_root = cross_cols(slope_two, second_root).astype(jnp.bfloat16)
    back_near = (cross_cols(slope_two, second_near) / divisor).astype(jnp.bfloat16)
    table_grad = cross_rows(root_pick, back_root) + cross_rows(multiples, back_near)
    pre_grad = (table_grad * (1.0 - jnp.exp(-hidden_table.astype(jnp.float32)))).astype(
        jnp.bfloat16
    )
    grad_one = jnp.dot(arrived, pre_grad, preferred_element_type=jnp.float32)
    grad_one = grad_one.astype(jnp.bfloat16)
    biases = jnp.stack(
        [
            jnp.sum(slope_two.astype(jnp.float32), axis=0),
            jnp.sum(pre_grad.astype(jnp.float32), axis=0),
        ]
    )
    rows_two, rows_one = grad_two.shape[0], grad_one.shape[0]
    units = -(-(rows_two + rows_one + 2) // owners_all)
    padding = units * owners_all - rows_two - rows_one
    biases = jnp.pad(biases.astype(jnp.bfloat16), ((0, padding - 2), (0, 0)))
    one, two = (units // 3) * owners_all, (2 * units // 3) * owners_all
    last = jnp.concatenate([grad_two[two:], grad_one, biases], axis=0)
    total = jnp.concatenate(
        sum_parts(
            [grad_two[:one], grad_two[one:two], last],
            [core + low + high + feat, core + high + feat + low, core + feat + low + high],
        ),
        axis=0,
    )
    half = rows_two // 2
    rootgrad_two = total[:half].astype(jnp.float32)
    neargrad_two = total[half:rows_two].astype(jnp.float32)
    grad_one = lax.dynamic_slice_in_dim(
        total[rows_two : rows_two + rows_one], place * depth, depth, 0
    ).astype(jnp.float32)
    rootgrad_one, neargrad_one = grad_one[:block_width], grad_one[block_width:]
    biasgrad_two = total[rows_two + rows_one].astype(jnp.float32)
    biasgrad_one = total[rows_two + rows_one + 1].astype(jnp.float32)
    return (
        layer_output,
        rootgrad_two,
        neargrad_two,
        biasgrad_two,
        rootgrad_one,
        neargrad_one,
        biasgrad_one,
    )


def solution(mesh):
    return jax.shard_map(
        local,
        mesh=mesh,
        in_specs=(
            P("feat", "trainer"),
            P("trainer", None),
            P("trainer"),
            P("trainer"),
            P("trainer"),
            P("feat", None),
            P("feat", None),
            P(),
            P(("feat", "trainer"), None),
            P(("feat", "trainer")),
            P(("feat", "trainer")),
            P(),
            P(),
            P(),
            P(("feat", "trainer"), None),
        ),
        out_specs=(
            P(("feat", "trainer"), None),
            P(),
            P(),
            P(),
            P("feat", None),
            P("feat", None),
            P(),
        ),
        check_vma=False,
    )
```
